32 devices in a mesh: row: 4 (over y, x), blk: 8 (over z, core).
Axes of the slice: x: 2, y: 2, z: 4, core: 2. Of those that a mesh axis runs over, the one named last changes fastest.
Arguments:
- spike_counts: int32 [16384, 2048], P(('row', 'blk')), may hold values from 0 to 23, as said below
- kernel_taps: int32 [16], replicated, may hold values from 1 to 8
- lag_bins: int32 [2], replicated, may hold values from 1 to 32, as said below
Outputs:
- correlogram: bfloat16 [2, 16384, 4, 4096], P(None, 'row', None, 'blk')
The draws below stay inside these ranges and needn't reach their ends.
Inputs may be any that keep to these rules, and one draw needn't show every extreme that they name: `spike_counts`: neurons fire at different rates and share a common drive. `lag_bins`: the second lag equals 32; the first lies between 1 and 31.
All inputs are finite; a program needn't handle non-finite values.
Results may differ from the reference program's by a relative error of at most 0.0034.
Values may be sent and summed in bfloat16 or wider, within the bound.
No kernel may reach another device: no remote copies, remote signals or barrier semaphores. Data moves between devices by JAX's collectives and lax.ppermute only.
A program may use at most 192 MiB of HBM per device.

```python
import jax
import jax.numpy as jnp
from jax import lax

NEURONS = 16384
BINS = 2048
TAPS = 16
LAGMAX = 32
PANEL = 4096
N_ROW = 4


def draw_spike_counts(key, part):
    key_rate = jax.random.fold_in(key, 11)
    key_noise = jax.random.fold_in(key, 12)
    key_drive = jax.random.fold_in(key, 13)
    key_share = jax.random.fold_in(key, 14)
    key_where = jax.random.fold_in(key, 15)
    position = jnp.arange(NEURONS, dtype=jnp.int32)[:, None]
    ceiling = 2 + jax.random.randint(key_rate, (NEURONS, 1), 0, 10) + 8 * position // NEURONS
    private = jax.random.randint(key_noise, (NEURONS, BINS), 0, ceiling)
    drive = jax.random.randint(key_drive, (1, BINS), 0, 4)
    share = jax.random.randint(key_share, (NEURONS, 1), 0, 3)
    counts = private + share * drive
    peak_row = jax.random.randint(jax.random.fold_in(key_where, 1), (), 0, NEURONS)
    peak_bin = jax.random.randint(jax.random.fold_in(key_where, 2), (), 0, BINS)
    bin_index = jnp.arange(BINS, dtype=jnp.int32)[None, :]
    counts = jnp.where((position == peak_row) & (bin_index == peak_bin), 23, counts)
    return counts.astype(jnp.int32)


def draw_lag_bins(key, part):
    first = jax.random.randint(jax.random.fold_in(key, 21), (1,), 1, LAGMAX)
    return jnp.concatenate([first, jnp.full((1,), LAGMAX, jnp.int32)]).astype(jnp.int32)


def touch_ends(entries, key, smallest, top_value):
    place = [jax.random.randint(jax.random.fold_in(key, axis), (), 0, length) for axis, length in enumerate(entries.shape)]
    widest = entries.shape.index(max(entries.shape))
    next_to = place[:widest] + [(place[widest] + 1) % entries.shape[widest]] + place[widest + 1:]
    return entries.at[tuple(place)].set(smallest).at[tuple(next_to)].set(top_value)


def setup_inputs(seed: int = 0) -> dict:
    key_of = jax.random.split(jax.random.key(seed), 4)
    return {
        "spike_counts": draw_spike_counts(jax.random.fold_in(key_of[3], 71), 0),
        "kernel_taps": touch_ends(jax.random.randint(key_of[1], (TAPS,), 1, 9), jax.random.fold_in(key_of[1], 1), 1, 8).astype(jnp.int32),
        "lag_bins": draw_lag_bins(jax.random.fold_in(key_of[3], 71), 0),
    }


def smoothed(spike_counts, kernel_taps):
    counts = spike_counts.astype(jnp.float32)
    weights = kernel_taps.astype(jnp.float32) / jnp.sum(kernel_taps.astype(jnp.float32))
    padded = jnp.pad(counts, ((0, 0), (TAPS - 1, 0)))
    result = jnp.zeros_like(counts)
    for delay in range(TAPS):
        result = result + weights[delay] * padded[:, TAPS - 1 - delay:TAPS - 1 - delay + BINS]
    return result

def reference(spike_counts, kernel_taps, lag_bins):
    smooth = smoothed(spike_counts, kernel_taps)
    centred = smooth - lax.optimization_barrier(jnp.mean(smooth, axis=1, keepdims=True))
    population = lax.optimization_barrier(jnp.mean(centred, axis=0))
    residual_part = centred - population[None, :]
    zscored = (residual_part * lax.rsqrt(lax.optimization_barrier(jnp.mean(residual_part * residual_part, axis=1, keepdims=True)) + 1e-05)).astype(jnp.bfloat16)
    zero_pad = jnp.pad(zscored, ((0, 0), (0, BINS)))
    panels = zscored.reshape(N_ROW, PANEL, BINS)
    results = []
    for which in range(2):
        shifted = lax.dynamic_slice_in_dim(zero_pad, lag_bins[which].astype(jnp.int32), BINS, 1)

        def one_panel(rows):
            return (jnp.dot(rows, shifted.T, preferred_element_type=jnp.float32) / BINS).astype(jnp.bfloat16)
        results.append(lax.map(one_panel, panels).reshape(NEURONS, NEURONS))
    return jnp.stack(results).reshape(2, NEURONS, N_ROW, PANEL)
```

```python
import functools

import jax
import jax.numpy as jnp
from jax import lax
from jax.experimental import pallas as pl
from jax.experimental.pallas import tpu as pltpu
from jax.sharding import PartitionSpec as P

NEURONS = 16384
BINS = 2048
TAPS = 16
AXES = ("row", "blk")
LANES = 128
BAND = 256
STEP = 64
MIB = 1 << 20
SCALE = 1.0


def smoothed(spike_counts, kernel_taps):
    counts = spike_counts.astype(jnp.float32)
    weights = kernel_taps.astype(jnp.float32) / jnp.sum(kernel_taps.astype(jnp.float32))
    padded = jnp.pad(counts, ((0, 0), (TAPS - 1, 0)))
    result = jnp.zeros_like(counts)
    for delay in range(TAPS):
        result = result + weights[delay] * padded[:, TAPS - 1 - delay : TAPS - 1 - delay + BINS]
    return result


def later_bins(data, lag):
    padded = jnp.pad(data, ((0, 0), (0, BINS)))
    return lax.dynamic_slice_in_dim(padded, lag, BINS, 1)


def gathered_shards(spike_counts, kernel_taps, lag_bins):
    smooth = smoothed(spike_counts, kernel_taps)
    centred = smooth - jnp.mean(smooth, axis=1, keepdims=True)
    totals = lax.psum(jnp.sum(centred, axis=0), AXES)
    residual_part = centred - (totals / NEURONS)[None, :]
    zscored = (
        residual_part
        * lax.rsqrt(jnp.mean(residual_part * residual_part, axis=1, keepdims=True) + 1e-05)
    ).astype(jnp.bfloat16)
    span_rows = zscored.shape[0]
    groups = lax.axis_size("row")
    columns = lax.all_gather(zscored, "row", axis=0, tiled=True)
    stacked = jnp.concatenate(
        [later_bins(columns, lag_bins[0]), later_bins(columns, lag_bins[1])], axis=0
    )
    piece = lax.all_gather(zscored, "blk", axis=0, tiled=True)
    product = jnp.dot(piece, stacked.T, preferred_element_type=jnp.float32) / BINS
    product = product.reshape(piece.shape[0], 2, groups, span_rows)
    return jnp.transpose(product, (1, 0, 2, 3)).astype(jnp.bfloat16)


def smooth_kernel(taps_ref, counts_ref, *out_refs):
    centred_refs, total_ref = out_refs[:2], out_refs[2]
    rows, bins = counts_ref.shape
    at = lax.broadcasted_iota(jnp.int32, (BAND, BAND), 1) - lax.broadcasted_iota(
        jnp.int32, (BAND, BAND), 0
    )
    same = jnp.zeros((BAND, BAND), jnp.float32)
    before = jnp.zeros((BAND, BAND), jnp.float32)
    weight = jnp.float32(0)
    for delay in range(TAPS):
        tap = taps_ref[delay].astype(jnp.float32)
        weight = weight + tap
        same = jnp.where(at == delay, tap, same)
        before = jnp.where(at == delay - BAND, tap, before)
    same = same.astype(jnp.bfloat16)
    before = before.astype(jnp.bfloat16)
    sums = []
    last = None
    for block in range(bins // BAND):
        part = counts_ref[:, block * BAND : (block + 1) * BAND].astype(jnp.float32)
        part = part.astype(jnp.bfloat16)
        filtered = jnp.dot(part, same, preferred_element_type=jnp.float32)
        if last is not None:
            filtered = filtered + jnp.dot(last, before, preferred_element_type=jnp.float32)
        sums.append(filtered)
        last = part
    mean = functools.reduce(
        jnp.add, [jnp.sum(filtered, axis=1, keepdims=True) for filtered in sums]
    ) * (1.0 / bins)
    for block, filtered in enumerate(sums):
        centred = (filtered - mean) / weight
        span = slice(block * BAND, (block + 1) * BAND)
        for number, centred_ref in enumerate(centred_refs):
            half = centred_ref.shape[0]
            centred_ref[:, span] = centred[number * half : (number + 1) * half].astype(
                jnp.bfloat16
            )
        total_ref[:, span] = jnp.sum(centred, axis=0, keepdims=True)


def smooth_rows(counts, taps):
    rows, bins = counts.shape
    half = jax.ShapeDtypeStruct((rows // 2, bins), jnp.bfloat16)
    return pl.pallas_call(
        smooth_kernel,
        in_specs=[
            pl.BlockSpec(memory_space=pltpu.SMEM),
            pl.BlockSpec(memory_space=pltpu.VMEM),
        ],
        out_specs=[pl.BlockSpec(memory_space=pltpu.VMEM)] * 3,
        out_shape=[half, half, jax.ShapeDtypeStruct((1, bins), jnp.float32)],
        compiler_params=pltpu.CompilerParams(vmem_limit_bytes=24 * MIB),
        cost_estimate=pl.CostEstimate(
            flops=int(SCALE * 4 * rows * bins * BAND), bytes_accessed=int(SCALE * 6 * rows * bins), transcendentals=0
        ),
        name="smooth_rows",
    )(taps, counts)


def standardized(centred, population):
    residual = centred.astype(jnp.float32) - population
    power = jnp.mean(residual * residual, axis=1, keepdims=True)
    return residual * lax.rsqrt(power + 1e-05)


def columns_kernel(counts, place_ref, lag_ref, population_ref, *refs):
    out_ref = refs[-1]
    population = population_ref[...]
    bins = population.shape[1]
    lane = lax.broadcasted_iota(jnp.int32, (STEP, LANES), 1)
    first = 0
    for turn, count in enumerate(counts):
        pieces = refs[first : first + count]
        first += count

        @pl.when(pl.program_id(0) == turn)
        def _():
            at = 0
            for piece in pieces:
                for start in range(0, piece.shape[0], STEP):
                    score = standardized(piece[start : start + STEP, :], population)
                    score = score.astype(jnp.bfloat16).astype(jnp.float32) * (1.0 / bins)
                    rows = slice(at % LANES, at % LANES + STEP)
                    for which in range(2):
                        lag = lag_ref[which]
                        after = jnp.zeros((STEP, LANES), jnp.float32)
                        for tile in reversed(range(bins // LANES)):
                            span = slice(tile * LANES, (tile + 1) * LANES)
                            moved = pltpu.roll(score[:, span], LANES - lag, 1)
                            merged = jnp.where(lane < LANES - lag, moved, after)
                            out_ref[which, at // LANES, 0, rows, span] = merged.astype(
                                jnp.bfloat16
                            )
                            after = moved
                    at += STEP


def column_groups(place, lag_bins, population, pieces, held, groups):
    bins = population.shape[1]
    tiles = sum(piece.shape[0] for piece in pieces[0]) // LANES
    flat = [piece for group in pieces for piece in group]
    whole = lambda i, place: (0, 0)
    in_specs = [pl.BlockSpec(memory_space=pltpu.SMEM), pl.BlockSpec((1, bins), whole)]
    in_specs += [pl.BlockSpec(piece.shape, whole) for piece in flat]
    operands = [lag_bins, population, *flat]
    aliases = {}
    if held is not None:
        in_specs.append(pl.BlockSpec(memory_space=pl.ANY))
        operands.append(held)
        aliases = {len(operands): 0}
    size = len(pieces) * tiles * LANES * bins
    return pl.pallas_call(
        functools.partial(columns_kernel, [len(group) for group in pieces]),
        grid_spec=pltpu.PrefetchScalarGridSpec(
            num_scalar_prefetch=1,
            grid=(len(pieces),),
            in_specs=in_specs,
            out_specs=pl.BlockSpec(
                (2, tiles, 1, LANES, bins), lambda i, place: (0, 0, place[i], 0, 0)
            ),
        ),
        out_shape=jax.ShapeDtypeStruct((2, tiles, groups, LANES, bins), jnp.bfloat16),
        input_output_aliases=aliases,
        compiler_params=pltpu.CompilerParams(vmem_limit_bytes=24 * MIB),
        cost_estimate=pl.CostEstimate(
            flops=int(SCALE * 12 * size), bytes_accessed=int(SCALE * 6 * size), transcendentals=0
        ),
        name="column_groups",
    )(place, *operands)


def product_kernel(count, wide, place_ref, spot_ref, population_ref, *refs):
    pieces = refs[:count]
    columns = refs[count : count + wide]
    out_ref, scores, mixed = refs[-3:]
    half, groups, lanes = out_ref.shape[-3:]
    halves = out_ref.shape[3]
    lag, tile = pl.program_id(0), pl.program_id(1)
    tiles = columns[0].shape[1]

    def standardize(number):
        population = population_ref[...]
        for start in range(0, half, STEP):
            at = pl.multiple_of(spot_ref[number] + start, STEP)
            scores[pl.ds(at, STEP), :] = standardized(
                pieces[number][start : start + STEP, :], population
            ).astype(jnp.bfloat16)

    def multiply(right, number):
        at = pl.multiple_of(spot_ref[number], half)
        product = lax.dot_general(
            scores[pl.ds(at, half), :],
            right,
            (((1,), (1,)), ((), ())),
            preferred_element_type=jnp.float32,
        )
        base = number * half * groups
        for group in range(groups):
            mixed[pl.ds(base + group, half, stride=groups), :] = product[
                :, group * lanes : (group + 1) * lanes
            ]
        done = mixed[base : base + half * groups, :].astype(jnp.bfloat16)
        block = spot_ref[number] // half
        out_ref[0, 0, block // halves, block % halves] = done.reshape(half, groups, lanes)

    def all_pieces(columns_ref, fresh):
        right = columns_ref[lag, tile % tiles].reshape(groups * lanes, columns_ref.shape[-1])
        if fresh:
            standardize(0)
        for number in range(count):
            if fresh and number + 1 < count:
                standardize(number + 1)
            multiply(right, number)

    fresh = (lag == 0) & (tile == 0)
    pl.when(fresh)(functools.partial(all_pieces, columns[0], True))
    for number in range(wide):
        mine = jnp.logical_not(fresh) & (tile // tiles == number)
        pl.when(mine)(functools.partial(all_pieces, columns[number], False))


def product_rows(place, spot, population, pieces, columns, which, held, shape):
    half, bins = pieces[0].shape
    halves = len(pieces) // 2
    wide = len(columns)
    _, tiles, groups, lanes, _ = columns[0].shape
    rows = half * len(pieces)
    operands = [population, *pieces, *columns]
    in_specs = [pl.BlockSpec(memory_space=pltpu.VMEM) for _ in operands]
    aliases = {}
    if held is not None:
        in_specs.append(pl.BlockSpec(memory_space=pl.ANY))
        operands.append(held)
        aliases = {2 + len(operands) - 1: 0}
    return pl.pallas_call(
        functools.partial(product_kernel, len(pieces), wide),
        grid_spec=pltpu.PrefetchScalarGridSpec(
            num_scalar_prefetch=2,
            grid=(2, wide * tiles),
            in_specs=in_specs,
            out_specs=pl.BlockSpec(
                (1, 1, 2, halves, half, groups, lanes),
                lambda l, k, place, spot: (l, place[0], 0, place[1], 0, 0, which * tiles + k),
            ),
            scratch_shapes=[
                pltpu.VMEM((rows, bins), jnp.bfloat16),
                pltpu.VMEM((rows * groups, lanes), jnp.float32),
            ],
        ),
        out_shape=jax.ShapeDtypeStruct(shape, jnp.bfloat16),
        input_output_aliases=aliases,
        compiler_params=pltpu.CompilerParams(vmem_limit_bytes=16 * MIB),
        cost_estimate=pl.CostEstimate(
            flops=int(SCALE * 4 * rows * wide * tiles * groups * lanes * bins),
            bytes_accessed=int(SCALE * 16 * MIB),
            transcendentals=0,
        ),
        name="product_rows",
    )(place, spot, *operands)


def pairs(target):
    found = []
    for row in range(4):
        for z in range(4):
            for core in range(2):
                to = target(row, z, core)
                if to is not None:
                    found.append((row * 8 + z * 2 + core, to[0] * 8 + to[1] * 2 + to[2]))
    return found


ACROSS_X = pairs(lambda row, z, core: (row ^ 1, z, core))
ACROSS_Y = pairs(lambda row, z, core: (row ^ 2, z, core))
ACROSS_BOTH = pairs(lambda row, z, core: (row ^ 3, z, core))
ALONG = [pairs(lambda row, z, core, n=n: (row, (z + n) % 4, core)) for n in (1, 2, 3)]
SIBLING = pairs(lambda row, z, core: (row, z, 1 - core))
OUTER = pairs(lambda row, z, core: (row, z ^ 1, core))
INNER = pairs(lambda row, z, core: (row, 3 - z, core) if z in (1, 2) else None)
OUTWARD = pairs(lambda row, z, core: (row, 0 if z == 1 else 3, core) if z in (1, 2) else None)


def send(data, route, name):
    with jax.named_scope(name):
        return lax.ppermute(data, AXES, route)


def line_shards(spike_counts, kernel_taps, lag_bins):
    rows, bins = spike_counts.shape
    half = rows // 2
    groups = lax.axis_size("row")
    row = lax.axis_index("row")
    z = lax.axis_index("blk") // 2
    core = lax.axis_index("blk") % 2
    inside = (z == 1) | (z == 2)
    low = z < 2

    *own, totals = smooth_rows(spike_counts, kernel_taps)

    parts = [send(totals, route, "sum_rows") for route in (ACROSS_X, ACROSS_Y, ACROSS_BOTH)]
    summed = totals + parts[0] + parts[1] + parts[2]
    summed = summed + send(summed, SIBLING, "sum_cores")
    parts = [send(summed, route, "sum_line") for route in ALONG]
    population = (summed + parts[0] + parts[1] + parts[2]) * (1.0 / NEURONS)

    near, far, sib, side, flank, corner = [], [], [], [], [], []
    for h in range(2):
        piece = own[h]
        if h == 1:
            piece, _ = lax.optimization_barrier((piece, summed))
        near.append(send(piece, OUTER, f"near_{h}"))
        far.append(send(piece, INNER, f"far_{h}"))
        sib.append(send(piece, SIBLING, f"sib_{h}"))
    for h in range(2):
        piece = own[h]
        if h == 1:
            piece, _ = lax.optimization_barrier((piece, corner[0]))
        side.append(send(piece, ACROSS_X, f"side_{h}"))
        flank.append(send(piece, ACROSS_Y, f"flank_{h}"))
        corner.append((side[h][: half // 2], flank[h][half // 2 :]))
    corner = [
        (send(a, ACROSS_Y, f"corner_{h}"), send(b, ACROSS_X, f"corner_{h}"))
        for h, (a, b) in enumerate(corner)
    ]

    far_near = [send(near[h], INNER, f"far_near_{h}") for h in range(2)]
    out_far = [send(far[h], OUTWARD, f"out_far_{h}") for h in range(2)]
    out_far_near = [send(far_near[h], OUTWARD, f"out_far_near_{h}") for h in range(2)]
    second = [jnp.where(inside, far[h], out_far[h]) for h in range(2)]
    third = [jnp.where(inside, far_near[h], out_far_near[h]) for h in range(2)]
    near_sib = [send(near[h], SIBLING, f"near_sib_{h}") for h in range(2)]
    second_sib = [send(second[h], SIBLING, f"second_sib_{h}") for h in range(2)]
    third_sib = [send(third[h], SIBLING, f"third_sib_{h}") for h in range(2)]

    place = jnp.stack([row, row ^ 1, row ^ 2, row ^ 3]).astype(jnp.int32)
    columns = []
    for h in range(2):
        part = column_groups(
            place[:3], lag_bins, population, [[own[h]], [side[h]], [flank[h]]], None, groups
        )
        part = column_groups(
            place[3:], lag_bins, population, [list(corner[h])], part, groups
        )
        columns.append(part)

    shape = (2, 4, 2, 2, half, groups, rows)
    mine, other = core * rows, (1 - core) * rows
    spot = jnp.stack([mine, mine + half, other, other + half]).astype(jnp.int32)
    spot_half = jnp.stack([core * half, (1 - core) * half]).astype(jnp.int32)

    def at(z, h):
        return jnp.stack([z, jnp.int32(h)]).astype(jnp.int32)

    out = None
    for h in range(2):
        for position, pieces in ((z, own + sib), (z ^ 1, near + near_sib)):
            out = product_rows(
                at(position, 0), spot, population, pieces, [columns[h]], h, out, shape
            )
    out = product_rows(
        at(jnp.where(low, 2, 1), 0),
        spot,
        population,
        second + second_sib,
        columns,
        0,
        out,
        shape,
    )
    for h in range(2):
        out = product_rows(
            at(jnp.where(low, 3, 0), h),
            spot_half,
            population,
            [third[h], third_sib[h]],
            columns,
            0,
            out,
            shape,
        )
    return out.reshape(2, 8 * rows, groups, rows)


def solution(mesh):
    placed = (P(("row", "blk"), None), P(), P())
    line = mesh.shape["row"] == 4 and mesh.shape["blk"] == 8
    return jax.shard_map(
        line_shards if line else gathered_shards,
        mesh=mesh,
        in_specs=placed,
        out_specs=P(None, "row", None, "blk"),
        check_vma=False,
    )
```

```python
import functools

import jax
import jax.numpy as jnp
from jax import lax
from jax.experimental import pallas as pl
from jax.experimental.pallas import tpu as pltpu
from jax.sharding import PartitionSpec as P

NEURONS = 16384
BINS = 2048
TAPS = 16
AXES = ("row", "blk")
LANES = 128
BAND = 256
STEP = 64
MIB = 1 << 20
SCALE = 1.0


def smoothed(spike_counts, kernel_taps):
    counts = spike_counts.astype(jnp.float32)
    weights = kernel_taps.astype(jnp.float32) / jnp.sum(kernel_taps.astype(jnp.float32))
    padded = jnp.pad(counts, ((0, 0), (TAPS - 1, 0)))
    result = jnp.zeros_like(counts)
    for delay in range(TAPS):
        result = result + weights[delay] * padded[:, TAPS - 1 - delay : TAPS - 1 - delay + BINS]
    return result


def later_bins(data, lag):
    padded = jnp.pad(data, ((0, 0), (0, BINS)))
    return lax.dynamic_slice_in_dim(padded, lag, BINS, 1)


def gathered_shards(spike_counts, kernel_taps, lag_bins):
    smooth = smoothed(spike_counts, kernel_taps)
    centred = smooth - jnp.mean(smooth, axis=1, keepdims=True)
    totals = lax.psum(jnp.sum(centred, axis=0), AXES)
    residual_part = centred - (totals / NEURONS)[None, :]
    zscored = (
        residual_part
        * lax.rsqrt(jnp.mean(residual_part * residual_part, axis=1, keepdims=True) + 1e-05)
    ).astype(jnp.bfloat16)
    span_rows = zscored.shape[0]
    groups = lax.axis_size("row")
    columns = lax.all_gather(zscored, "row", axis=0, tiled=True)
    stacked = jnp.concatenate(
        [later_bins(columns, lag_bins[0]), later_bins(columns, lag_bins[1])], axis=0
    )
    piece = lax.all_gather(zscored, "blk", axis=0, tiled=True)
    product = jnp.dot(piece, stacked.T, preferred_element_type=jnp.float32) / BINS
    product = product.reshape(piece.shape[0], 2, groups, span_rows)
    return jnp.transpose(product, (1, 0, 2, 3)).astype(jnp.bfloat16)


def smooth_kernel(spans, taps_ref, counts_ref, *out_refs):
    centred_refs, total_ref = out_refs[:-1], out_refs[-1]
    rows, bins = counts_ref.shape
    at = lax.broadcasted_iota(jnp.int32, (BAND, BAND), 1) - lax.broadcasted_iota(
        jnp.int32, (BAND, BAND), 0
    )
    same = jnp.zeros((BAND, BAND), jnp.float32)
    before = jnp.zeros((BAND, BAND), jnp.float32)
    weight = jnp.float32(0)
    for delay in range(TAPS):
        tap = taps_ref[delay].astype(jnp.float32)
        weight = weight + tap
        same = jnp.where(at == delay, tap, same)
        before = jnp.where(at == delay - BAND, tap, before)
    same = same.astype(jnp.bfloat16)
    before = before.astype(jnp.bfloat16)
    sums = []
    last = None
    for block in range(bins // BAND):
        part = counts_ref[:, block * BAND : (block + 1) * BAND].astype(jnp.float32)
        part = part.astype(jnp.bfloat16)
        filtered = jnp.dot(part, same, preferred_element_type=jnp.float32)
        if last is not None:
            filtered = filtered + jnp.dot(last, before, preferred_element_type=jnp.float32)
        sums.append(filtered)
        last = part
    mean = functools.reduce(
        jnp.add, [jnp.sum(filtered, axis=1, keepdims=True) for filtered in sums]
    ) * (1.0 / bins)
    for block, filtered in enumerate(sums):
        centred = (filtered - mean) / weight
        span = slice(block * BAND, (block + 1) * BAND)
        rounded = centred.astype(jnp.bfloat16)
        for (start, stop), centred_ref in zip(spans, centred_refs):
            centred_ref[:, span] = rounded[start:stop]
        total_ref[:, span] = jnp.sum(centred, axis=0, keepdims=True)


def smooth_rows(counts, taps, spans):
    rows, bins = counts.shape
    shapes = [jax.ShapeDtypeStruct((stop - start, bins), jnp.bfloat16) for start, stop in spans]
    return pl.pallas_call(
        functools.partial(smooth_kernel, spans),
        in_specs=[
            pl.BlockSpec(memory_space=pltpu.SMEM),
            pl.BlockSpec(memory_space=pltpu.VMEM),
        ],
        out_specs=[pl.BlockSpec(memory_space=pltpu.VMEM)] * (len(spans) + 1),
        out_shape=[*shapes, jax.ShapeDtypeStruct((1, bins), jnp.float32)],
        compiler_params=pltpu.CompilerParams(vmem_limit_bytes=24 * MIB),
        cost_estimate=pl.CostEstimate(
            flops=int(SCALE * 4 * rows * bins * BAND), bytes_accessed=int(SCALE * 6 * rows * bins), transcendentals=0
        ),
        name="smooth_rows",
    )(taps, counts)


def standardized(centred, population):
    residual = centred.astype(jnp.float32) - population
    power = jnp.mean(residual * residual, axis=1, keepdims=True)
    return residual * lax.rsqrt(power + 1e-05)


def scores_kernel(population_ref, *refs):
    population = population_ref[...]
    at = 0
    for piece in refs[:-1]:
        for start in range(0, piece.shape[0], STEP):
            refs[-1][at : at + STEP, :] = standardized(
                piece[start : start + STEP, :], population
            ).astype(jnp.bfloat16)
            at += STEP


def scores(population, pieces):
    rows, bins = sum(piece.shape[0] for piece in pieces), pieces[0].shape[1]
    return pl.pallas_call(
        scores_kernel,
        in_specs=[pl.BlockSpec(memory_space=pltpu.VMEM)] * (1 + len(pieces)),
        out_specs=pl.BlockSpec(memory_space=pltpu.VMEM),
        out_shape=jax.ShapeDtypeStruct((rows, bins), jnp.bfloat16),
        compiler_params=pltpu.CompilerParams(vmem_limit_bytes=16 * MIB),
        cost_estimate=pl.CostEstimate(
            flops=int(SCALE * 6 * rows * bins),
            bytes_accessed=int(SCALE * 4 * rows * bins),
            transcendentals=0,
        ),
        name="scores",
    )(population, *pieces)


def columns_kernel(counts, place_ref, lag_ref, population_ref, *refs):
    out_ref = refs[-1]
    population = population_ref[...]
    bins = population.shape[1]
    lane = lax.broadcasted_iota(jnp.int32, (STEP, LANES), 1)
    first = 0
    for turn, count in enumerate(counts):
        pieces = refs[first : first + count]
        first += count

        @pl.when(pl.program_id(0) == turn)
        def _():
            at = 0
            for piece in pieces:
                for start in range(0, piece.shape[0], STEP):
                    score = standardized(piece[start : start + STEP, :], population)
                    score = score.astype(jnp.bfloat16).astype(jnp.float32) * (1.0 / bins)
                    rows = slice(at % LANES, at % LANES + STEP)
                    for which in range(2):
                        lag = lag_ref[which]
                        after = jnp.zeros((STEP, LANES), jnp.float32)
                        for tile in reversed(range(bins // LANES)):
                            span = slice(tile * LANES, (tile + 1) * LANES)
                            moved = pltpu.roll(score[:, span], LANES - lag, 1)
                            merged = jnp.where(lane < LANES - lag, moved, after)
                            out_ref[which, at // LANES, 0, rows, span] = merged.astype(
                                jnp.bfloat16
                            )
                            after = moved
                    at += STEP


def column_groups(place, lag_bins, population, pieces, held, groups):
    bins = population.shape[1]
    tiles = sum(piece.shape[0] for piece in pieces[0]) // LANES
    flat = [piece for group in pieces for piece in group]
    in_specs = [pl.BlockSpec(memory_space=pltpu.SMEM)]
    in_specs += [pl.BlockSpec(memory_space=pltpu.VMEM)] * (1 + len(flat))
    operands = [lag_bins, population, *flat]
    aliases = {}
    if held is not None:
        in_specs.append(pl.BlockSpec(memory_space=pl.ANY))
        operands.append(held)
        aliases = {len(operands): 0}
    size = len(pieces) * tiles * LANES * bins
    return pl.pallas_call(
        functools.partial(columns_kernel, [len(group) for group in pieces]),
        grid_spec=pltpu.PrefetchScalarGridSpec(
            num_scalar_prefetch=1,
            grid=(len(pieces),),
            in_specs=in_specs,
            out_specs=pl.BlockSpec(
                (2, tiles, 1, LANES, bins), lambda i, place: (0, 0, place[i], 0, 0)
            ),
        ),
        out_shape=jax.ShapeDtypeStruct((2, tiles, groups, LANES, bins), jnp.bfloat16),
        input_output_aliases=aliases,
        compiler_params=pltpu.CompilerParams(vmem_limit_bytes=14 * MIB),
        cost_estimate=pl.CostEstimate(
            flops=int(SCALE * 12 * size), bytes_accessed=int(SCALE * 6 * size), transcendentals=0
        ),
        name="column_groups",
    )(place, *operands)


def product_kernel(offsets, starts, ready, place_ref, spot_ref, population_ref, *refs):
    count, wide = len(offsets), len(starts)
    pieces = refs[:count]
    out_ref, mixed, scores, raw, sems = refs[-5:]
    halves, half, groups, lanes = out_ref.shape[-4:]
    columns = refs[count : count + wide]
    lag, tile = pl.program_id(0), pl.program_id(1)

    def copy(number):
        source = pieces[number].at[pl.ds(offsets[number], half), :]
        into = scores.at[pl.ds(number * half, half), :] if ready else raw.at[number]
        return pltpu.make_async_copy(source, into, sems.at[number])

    def prepare(number):
        copy(number).wait()
        if not ready:
            population = population_ref[...]
            for start in range(0, half, STEP):
                at = number * half + start
                scores[at : at + STEP, :] = standardized(
                    raw[number, start : start + STEP, :], population
                ).astype(jnp.bfloat16)

    def multiply(right, number):
        product = lax.dot_general(
            scores[number * half : (number + 1) * half, :],
            right,
            (((1,), (1,)), ((), ())),
            preferred_element_type=jnp.float32,
        )
        base = number * half * groups
        for group in range(groups):
            mixed[pl.ds(base + group, half, stride=groups), :] = product[
                :, group * lanes : (group + 1) * lanes
            ]
        done = mixed[base : base + half * groups, :].astype(jnp.bfloat16)
        block = spot_ref[number]
        out_ref[0, 0, block // halves, block % halves] = done.reshape(half, groups, lanes)

    def all_pieces(columns_ref, start, fresh):
        right = columns_ref[lag, tile - start].reshape(groups * lanes, columns_ref.shape[-1])
        if fresh:
            for number in range(count):
                copy(number).start()
            prepare(0)
        for number in range(count):
            if fresh and number + 1 < count:
                prepare(number + 1)
            multiply(right, number)

    fresh = (lag == 0) & (tile == 0)
    pl.when(fresh)(functools.partial(all_pieces, columns[0], 0, True))
    for columns_ref, start in zip(columns, starts):
        mine = (tile >= start) & (tile < start + columns_ref.shape[1])
        mine = mine & jnp.logical_not(fresh)
        pl.when(mine)(functools.partial(all_pieces, columns_ref, start, False))


def product_rows(place, spot, population, pieces, half, columns, which, held, shape, ready=False):
    arrays, offsets = zip(*pieces)
    bins = arrays[0].shape[1]
    halves = len(pieces) // 2
    wide = len(columns)
    _, _, groups, lanes, _ = columns[0].shape
    counts = [column.shape[1] for column in columns]
    starts = [sum(counts[:number]) for number in range(wide)]
    tiles = sum(counts)
    rows = half * len(pieces)
    operands = [population, *arrays, *columns]
    in_specs = [pl.BlockSpec(memory_space=pltpu.VMEM)]
    in_specs += [pl.BlockSpec(memory_space=pl.ANY) for _ in pieces]
    in_specs += [pl.BlockSpec(memory_space=pltpu.VMEM) for _ in columns]
    aliases = {}
    if held is not None:
        in_specs.append(pl.BlockSpec(memory_space=pl.ANY))
        operands.append(held)
        aliases = {2 + len(operands) - 1: 0}
    return pl.pallas_call(
        functools.partial(product_kernel, offsets, starts, ready),
        grid_spec=pltpu.PrefetchScalarGridSpec(
            num_scalar_prefetch=2,
            grid=(2, tiles),
            in_specs=in_specs,
            out_specs=pl.BlockSpec(
                (1, 1, 2, halves, half, groups, lanes),
                lambda l, k, place, spot: (l, place[0], 0, place[1], 0, 0, which + k),
            ),
            scratch_shapes=[
                pltpu.VMEM((rows * groups, lanes), jnp.float32),
                pltpu.VMEM((rows, bins), jnp.bfloat16),
                pltpu.VMEM((1 if ready else len(pieces), half, bins), jnp.bfloat16),
                pltpu.SemaphoreType.DMA((len(pieces),)),
            ],
        ),
        out_shape=jax.ShapeDtypeStruct(shape, jnp.bfloat16),
        input_output_aliases=aliases,
        compiler_params=pltpu.CompilerParams(vmem_limit_bytes=22 * MIB),
        cost_estimate=pl.CostEstimate(
            flops=int(SCALE * 4 * rows * tiles * groups * lanes * bins),
            bytes_accessed=int(SCALE * 16 * MIB),
            transcendentals=0,
        ),
        name="product_rows",
    )(place, spot, *operands)


def pairs(target):
    found = []
    for row in range(4):
        for z in range(4):
            for core in range(2):
                to = target(row, z, core)
                if to is not None:
                    found.append((row * 8 + z * 2 + core, to[0] * 8 + to[1] * 2 + to[2]))
    return found


ACROSS_X = pairs(lambda row, z, core: (row ^ 1, z, core))
ACROSS_Y = pairs(lambda row, z, core: (row ^ 2, z, core))
ACROSS_BOTH = pairs(lambda row, z, core: (row ^ 3, z, core))
ALONG = [pairs(lambda row, z, core, n=n: (row, (z + n) % 4, core)) for n in (1, 2, 3)]
SIBLING = pairs(lambda row, z, core: (row, z, 1 - core))
OUTER = pairs(lambda row, z, core: (row, z ^ 1, core))
INNER = pairs(lambda row, z, core: (row, 3 - z, core) if z in (1, 2) else None)
OUTWARD = pairs(lambda row, z, core: (row, 0 if z == 1 else 3, core) if z in (1, 2) else None)


def send(data, route, name):
    with jax.named_scope(name):
        return lax.ppermute(data, AXES, route)


def line_shards(spike_counts, kernel_taps, lag_bins):
    rows, bins = spike_counts.shape
    half = rows // 2
    groups = lax.axis_size("row")
    row = lax.axis_index("row")
    z = lax.axis_index("blk") // 2
    core = lax.axis_index("blk") % 2
    inside = (z == 1) | (z == 2)
    low = z < 2

    shard, totals = smooth_rows(spike_counts, kernel_taps, [(0, rows)])

    def after(data, *events):
        return lax.optimization_barrier((data, *events))[0]

    parts = [send(totals, route, "sum_line") for route in ALONG]
    line_total = totals + parts[0] + parts[1] + parts[2]
    piece = after(shard, line_total)
    near = send(piece, OUTER, "near")
    far = send(piece, INNER, "far")
    side = send(piece, ACROSS_X, "side")
    flank = send(piece, ACROSS_Y, "flank")
    pair_total = line_total + send(line_total, SIBLING, "sum_cores")
    sib = send(after(shard, pair_total), SIBLING, "sib")
    summed = pair_total + send(after(pair_total, sib), ACROSS_X, "sum_x")
    summed = summed + send(summed, ACROSS_Y, "sum_y")
    population = summed * (1.0 / NEURONS)

    out_far = send(far, OUTWARD, "out_far")
    far_near = send(near, INNER, "far_near")
    corner = [
        send(after(side, population)[:half], ACROSS_Y, "corner"),
        send(after(flank, population)[half:], ACROSS_X, "corner"),
    ]
    near_sib = send(near, SIBLING, "near_sib")

    place = jnp.stack([row, row ^ 1, row ^ 2, row ^ 3]).astype(jnp.int32)
    part = column_groups(
        place[:3], lag_bins, population, [[shard], [side], [flank]], None, groups
    )
    own_rows = scores(after(population, part), [shard, sib])
    near_rows = scores(after(population, own_rows), [near, near_sib])
    columns = column_groups(
        place[3:], lag_bins, population, [corner], after(part, near_rows), groups
    )

    spot = jnp.stack([core * 2, core * 2 + 1, 2 - core * 2, 3 - core * 2]).astype(jnp.int32)
    shape = (2, 4, 2, 2, half, groups, rows)

    def products(position, pieces, held, ready):
        return product_rows(
            jnp.stack([position, jnp.int32(0)]).astype(jnp.int32),
            spot,
            population,
            [(piece, at) for piece in pieces for at in range(0, piece.shape[0], half)],
            half,
            [columns],
            0,
            held,
            shape,
            ready,
        )

    out = products(z, [own_rows], None, True)
    out_far_near = send(after(far_near, out), OUTWARD, "out_far_near")
    second = jnp.where(inside, far, after(out_far, out))
    second_sib = send(second, SIBLING, "second_sib")
    out = products(z ^ 1, [near_rows], out, True)
    out = products(jnp.where(low, 2, 1), [second, second_sib], out, False)
    third = jnp.where(inside, far_near, after(out_far_near, out))
    third_sib = send(third, SIBLING, "third_sib")
    out = products(jnp.where(low, 3, 0), [third, third_sib], out, False)
    return out.reshape(2, 8 * rows, groups, rows)


def solution(mesh):
    placed = (P(("row", "blk"), None), P(), P())
    line = mesh.shape["row"] == 4 and mesh.shape["blk"] == 8
    return jax.shard_map(
        line_shards if line else gathered_shards,
        mesh=mesh,
        in_specs=placed,
        out_specs=P(None, "row", None, "blk"),
        check_vma=False,
    )
```

```python
import functools

import jax
import jax.numpy as jnp
from jax import lax
from jax.experimental import pallas as pl
from jax.experimental.pallas import tpu as pltpu
from jax.sharding import PartitionSpec as P

NEURONS = 16384
BINS = 2048
TAPS = 16
AXES = ("row", "blk")
LANES = 128
BAND = 256
STEP = 64
MIB = 1 << 20
SCALE = 0.3


def smoothed(spike_counts, kernel_taps):
    counts = spike_counts.astype(jnp.float32)
    weights = kernel_taps.astype(jnp.float32) / jnp.sum(kernel_taps.astype(jnp.float32))
    padded = jnp.pad(counts, ((0, 0), (TAPS - 1, 0)))
    result = jnp.zeros_like(counts)
    for delay in range(TAPS):
        result = result + weights[delay] * padded[:, TAPS - 1 - delay : TAPS - 1 - delay + BINS]
    return result


def later_bins(data, lag):
    padded = jnp.pad(data, ((0, 0), (0, BINS)))
    return lax.dynamic_slice_in_dim(padded, lag, BINS, 1)


def gathered_shards(spike_counts, kernel_taps, lag_bins):
    smooth = smoothed(spike_counts, kernel_taps)
    centred = smooth - jnp.mean(smooth, axis=1, keepdims=True)
    totals = lax.psum(jnp.sum(centred, axis=0), AXES)
    residual_part = centred - (totals / NEURONS)[None, :]
    zscored = (
        residual_part
        * lax.rsqrt(jnp.mean(residual_part * residual_part, axis=1, keepdims=True) + 1e-05)
    ).astype(jnp.bfloat16)
    span_rows = zscored.shape[0]
    groups = lax.axis_size("row")
    columns = lax.all_gather(zscored, "row", axis=0, tiled=True)
    stacked = jnp.concatenate(
        [later_bins(columns, lag_bins[0]), later_bins(columns, lag_bins[1])], axis=0
    )
    piece = lax.all_gather(zscored, "blk", axis=0, tiled=True)
    product = jnp.dot(piece, stacked.T, preferred_element_type=jnp.float32) / BINS
    product = product.reshape(piece.shape[0], 2, groups, span_rows)
    return jnp.transpose(product, (1, 0, 2, 3)).astype(jnp.bfloat16)


def smooth_kernel(spans, taps_ref, counts_ref, *out_refs):
    centred_refs, total_ref = out_refs[:-1], out_refs[-1]
    rows, bins = counts_ref.shape
    at = lax.broadcasted_iota(jnp.int32, (BAND, BAND), 1) - lax.broadcasted_iota(
        jnp.int32, (BAND, BAND), 0
    )
    same = jnp.zeros((BAND, BAND), jnp.float32)
    before = jnp.zeros((BAND, BAND), jnp.float32)
    weight = jnp.float32(0)
    for delay in range(TAPS):
        tap = taps_ref[delay].astype(jnp.float32)
        weight = weight + tap
        same = jnp.where(at == delay, tap, same)
        before = jnp.where(at == delay - BAND, tap, before)
    same = same.astype(jnp.bfloat16)
    before = before.astype(jnp.bfloat16)
    sums = []
    last = None
    for block in range(bins // BAND):
        part = counts_ref[:, block * BAND : (block + 1) * BAND].astype(jnp.float32)
        part = part.astype(jnp.bfloat16)
        filtered = jnp.dot(part, same, preferred_element_type=jnp.float32)
        if last is not None:
            filtered = filtered + jnp.dot(last, before, preferred_element_type=jnp.float32)
        sums.append(filtered)
        last = part
    mean = functools.reduce(
        jnp.add, [jnp.sum(filtered, axis=1, keepdims=True) for filtered in sums]
    ) * (1.0 / bins)
    for block, filtered in enumerate(sums):
        centred = (filtered - mean) / weight
        span = slice(block * BAND, (block + 1) * BAND)
        rounded = centred.astype(jnp.bfloat16)
        for (start, stop), centred_ref in zip(spans, centred_refs):
            centred_ref[:, span] = rounded[start:stop]
        total_ref[:, span] = jnp.sum(centred, axis=0, keepdims=True)


def smooth_rows(counts, taps, spans):
    rows, bins = counts.shape
    shapes = [jax.ShapeDtypeStruct((stop - start, bins), jnp.bfloat16) for start, stop in spans]
    return pl.pallas_call(
        functools.partial(smooth_kernel, spans),
        in_specs=[
            pl.BlockSpec(memory_space=pltpu.SMEM),
            pl.BlockSpec(memory_space=pltpu.VMEM),
        ],
        out_specs=[pl.BlockSpec(memory_space=pltpu.VMEM)] * (len(spans) + 1),
        out_shape=[*shapes, jax.ShapeDtypeStruct((1, bins), jnp.float32)],
        compiler_params=pltpu.CompilerParams(vmem_limit_bytes=24 * MIB),
        cost_estimate=pl.CostEstimate(
            flops=int(SCALE * 4 * rows * bins * BAND), bytes_accessed=int(SCALE * 6 * rows * bins), transcendentals=0
        ),
        name="smooth_rows",
    )(taps, counts)


def standardized(centred, population):
    residual = centred.astype(jnp.float32) - population
    power = jnp.mean(residual * residual, axis=1, keepdims=True)
    return residual * lax.rsqrt(power + 1e-05)


def scores_kernel(population_ref, *refs):
    population = population_ref[...]
    at = 0
    for piece in refs[:-1]:
        for start in range(0, piece.shape[0], STEP):
            refs[-1][at : at + STEP, :] = standardized(
                piece[start : start + STEP, :], population
            ).astype(jnp.bfloat16)
            at += STEP


def scores(population, pieces):
    rows, bins = sum(piece.shape[0] for piece in pieces), pieces[0].shape[1]
    return pl.pallas_call(
        scores_kernel,
        in_specs=[pl.BlockSpec(memory_space=pltpu.VMEM)] * (1 + len(pieces)),
        out_specs=pl.BlockSpec(memory_space=pltpu.VMEM),
        out_shape=jax.ShapeDtypeStruct((rows, bins), jnp.bfloat16),
        compiler_params=pltpu.CompilerParams(vmem_limit_bytes=16 * MIB),
        cost_estimate=pl.CostEstimate(
            flops=int(SCALE * 6 * rows * bins),
            bytes_accessed=int(SCALE * 4 * rows * bins),
            transcendentals=0,
        ),
        name="scores",
    )(population, *pieces)


def columns_kernel(counts, place_ref, lag_ref, population_ref, *refs):
    out_ref = refs[-1]
    population = population_ref[...]
    bins = population.shape[1]
    lane = lax.broadcasted_iota(jnp.int32, (STEP, LANES), 1)
    first = 0
    for turn, count in enumerate(counts):
        pieces = refs[first : first + count]
        first += count

        @pl.when(pl.program_id(0) == turn)
        def _():
            at = 0
            for piece in pieces:
                for start in range(0, piece.shape[0], STEP):
                    score = standardized(piece[start : start + STEP, :], population)
                    score = score.astype(jnp.bfloat16).astype(jnp.float32) * (1.0 / bins)
                    rows = slice(at % LANES, at % LANES + STEP)
                    for which in range(2):
                        lag = lag_ref[which]
                        after = jnp.zeros((STEP, LANES), jnp.float32)
                        for tile in reversed(range(bins // LANES)):
                            span = slice(tile * LANES, (tile + 1) * LANES)
                            moved = pltpu.roll(score[:, span], LANES - lag, 1)
                            merged = jnp.where(lane < LANES - lag, moved, after)
                            out_ref[which, at // LANES, 0, rows, span] = merged.astype(
                                jnp.bfloat16
                            )
                            after = moved
                    at += STEP


def column_groups(place, lag_bins, population, pieces, held, groups):
    bins = population.shape[1]
    tiles = sum(piece.shape[0] for piece in pieces[0]) // LANES
    flat = [piece for group in pieces for piece in group]
    in_specs = [pl.BlockSpec(memory_space=pltpu.SMEM)]
    in_specs += [pl.BlockSpec(memory_space=pltpu.VMEM)] * (1 + len(flat))
    operands = [lag_bins, population, *flat]
    aliases = {}
    if held is not None:
        in_specs.append(pl.BlockSpec(memory_space=pl.ANY))
        operands.append(held)
        aliases = {len(operands): 0}
    size = len(pieces) * tiles * LANES * bins
    return pl.pallas_call(
        functools.partial(columns_kernel, [len(group) for group in pieces]),
        grid_spec=pltpu.PrefetchScalarGridSpec(
            num_scalar_prefetch=1,
            grid=(len(pieces),),
            in_specs=in_specs,
            out_specs=pl.BlockSpec(
                (2, tiles, 1, LANES, bins), lambda i, place: (0, 0, place[i], 0, 0)
            ),
        ),
        out_shape=jax.ShapeDtypeStruct((2, tiles, groups, LANES, bins), jnp.bfloat16),
        input_output_aliases=aliases,
        compiler_params=pltpu.CompilerParams(vmem_limit_bytes=14 * MIB),
        cost_estimate=pl.CostEstimate(
            flops=int(SCALE * 12 * size), bytes_accessed=int(SCALE * 6 * size), transcendentals=0
        ),
        name="column_groups",
    )(place, *operands)


def product_kernel(offsets, starts, ready, place_ref, spot_ref, population_ref, *refs):
    count, wide = len(offsets), len(starts)
    pieces = refs[:count]
    out_ref, mixed, scores, raw, sems = refs[-5:]
    halves, half, groups, lanes = out_ref.shape[-4:]
    columns = refs[count : count + wide]
    lag, tile = pl.program_id(0), pl.program_id(1)

    def copy(number):
        source = pieces[number].at[pl.ds(offsets[number], half), :]
        into = scores.at[pl.ds(number * half, half), :] if ready else raw.at[number]
        return pltpu.make_async_copy(source, into, sems.at[number])

    def prepare(number):
        copy(number).wait()
        if not ready:
            population = population_ref[...]
            for start in range(0, half, STEP):
                at = number * half + start
                scores[at : at + STEP, :] = standardized(
                    raw[number, start : start + STEP, :], population
                ).astype(jnp.bfloat16)

    def multiply(right, number):
        product = lax.dot_general(
            scores[number * half : (number + 1) * half, :],
            right,
            (((1,), (1,)), ((), ())),
            preferred_element_type=jnp.float32,
        )
        base = number * half * groups
        for group in range(groups):
            mixed[pl.ds(base + group, half, stride=groups), :] = product[
                :, group * lanes : (group + 1) * lanes
            ]
        done = mixed[base : base + half * groups, :].astype(jnp.bfloat16)
        block = spot_ref[number]
        out_ref[0, 0, block // halves, block % halves] = done.reshape(half, groups, lanes)

    def all_pieces(columns_ref, start, fresh):
        right = columns_ref[lag, tile - start].reshape(groups * lanes, columns_ref.shape[-1])
        if fresh:
            for number in range(count):
                copy(number).start()
            prepare(0)
        for number in range(count):
            if fresh and number + 1 < count:
                prepare(number + 1)
            multiply(right, number)

    fresh = (lag == 0) & (tile == 0)
    pl.when(fresh)(functools.partial(all_pieces, columns[0], 0, True))
    for columns_ref, start in zip(columns, starts):
        mine = (tile >= start) & (tile < start + columns_ref.shape[1])
        mine = mine & jnp.logical_not(fresh)
        pl.when(mine)(functools.partial(all_pieces, columns_ref, start, False))


def product_rows(place, spot, population, pieces, half, columns, which, held, shape, ready=False):
    arrays, offsets = zip(*pieces)
    bins = arrays[0].shape[1]
    halves = len(pieces) // 2
    wide = len(columns)
    _, _, groups, lanes, _ = columns[0].shape
    counts = [column.shape[1] for column in columns]
    starts = [sum(counts[:number]) for number in range(wide)]
    tiles = sum(counts)
    rows = half * len(pieces)
    operands = [population, *arrays, *columns]
    in_specs = [pl.BlockSpec(memory_space=pltpu.VMEM)]
    in_specs += [pl.BlockSpec(memory_space=pl.ANY) for _ in pieces]
    in_specs += [pl.BlockSpec(memory_space=pltpu.VMEM) for _ in columns]
    aliases = {}
    if held is not None:
        in_specs.append(pl.BlockSpec(memory_space=pl.ANY))
        operands.append(held)
        aliases = {2 + len(operands) - 1: 0}
    return pl.pallas_call(
        functools.partial(product_kernel, offsets, starts, ready),
        grid_spec=pltpu.PrefetchScalarGridSpec(
            num_scalar_prefetch=2,
            grid=(2, tiles),
            in_specs=in_specs,
            out_specs=pl.BlockSpec(
                (1, 1, 2, halves, half, groups, lanes),
                lambda l, k, place, spot: (l, place[0], 0, place[1], 0, 0, which + k),
            ),
            scratch_shapes=[
                pltpu.VMEM((rows * groups, lanes), jnp.float32),
                pltpu.VMEM((rows, bins), jnp.bfloat16),
                pltpu.VMEM((1 if ready else len(pieces), half, bins), jnp.bfloat16),
                pltpu.SemaphoreType.DMA((len(pieces),)),
            ],
        ),
        out_shape=jax.ShapeDtypeStruct(shape, jnp.bfloat16),
        input_output_aliases=aliases,
        compiler_params=pltpu.CompilerParams(vmem_limit_bytes=22 * MIB),
        cost_estimate=pl.CostEstimate(
            flops=int(SCALE * 4 * rows * tiles * groups * lanes * bins),
            bytes_accessed=int(SCALE * 16 * MIB),
            transcendentals=0,
        ),
        name="product_rows",
    )(place, spot, *operands)


def pairs(target):
    found = []
    for row in range(4):
        for z in range(4):
            for core in range(2):
                to = target(row, z, core)
                if to is not None:
                    found.append((row * 8 + z * 2 + core, to[0] * 8 + to[1] * 2 + to[2]))
    return found


ACROSS_X = pairs(lambda row, z, core: (row ^ 1, z, core))
ACROSS_Y = pairs(lambda row, z, core: (row ^ 2, z, core))
ACROSS_BOTH = pairs(lambda row, z, core: (row ^ 3, z, core))
ALONG = [pairs(lambda row, z, core, n=n: (row, (z + n) % 4, core)) for n in (1, 2, 3)]
SIBLING = pairs(lambda row, z, core: (row, z, 1 - core))
OUTER = pairs(lambda row, z, core: (row, z ^ 1, core))
INNER = pairs(lambda row, z, core: (row, 3 - z, core) if z in (1, 2) else None)
OUTWARD = pairs(lambda row, z, core: (row, 0 if z == 1 else 3, core) if z in (1, 2) else None)


def send(data, route, name):
    with jax.named_scope(name):
        return lax.ppermute(data, AXES, route)


def line_shards(spike_counts, kernel_taps, lag_bins):
    rows, bins = spike_counts.shape
    half = rows // 2
    groups = lax.axis_size("row")
    row = lax.axis_index("row")
    z = lax.axis_index("blk") // 2
    core = lax.axis_index("blk") % 2
    inside = (z == 1) | (z == 2)
    low = z < 2

    shard, totals = smooth_rows(spike_counts, kernel_taps, [(0, rows)])

    def after(data, *events):
        return lax.optimization_barrier((data, *events))[0]

    parts = [send(totals, route, "sum_line") for route in ALONG]
    line_total = totals + parts[0] + parts[1] + parts[2]
    piece = after(shard, line_total)
    near = send(piece, OUTER, "near")
    far = send(piece, INNER, "far")
    side = send(piece, ACROSS_X, "side")
    flank = send(piece, ACROSS_Y, "flank")
    pair_total = line_total + send(line_total, SIBLING, "sum_cores")
    sib = send(after(shard, pair_total), SIBLING, "sib")
    summed = pair_total + send(after(pair_total, sib), ACROSS_X, "sum_x")
    summed = summed + send(summed, ACROSS_Y, "sum_y")
    population = summed * (1.0 / NEURONS)

    out_far = send(far, OUTWARD, "out_far")
    far_near = send(near, INNER, "far_near")
    corner = [
        send(after(side, population)[:half], ACROSS_Y, "corner"),
        send(after(flank, population)[half:], ACROSS_X, "corner"),
    ]
    near_sib = send(near, SIBLING, "near_sib")

    place = jnp.stack([row, row ^ 1, row ^ 2, row ^ 3]).astype(jnp.int32)
    part = column_groups(
        place[:3], lag_bins, population, [[shard], [side], [flank]], None, groups
    )
    own_rows = scores(after(population, part), [shard, sib])
    near_rows = scores(after(population, own_rows), [near, near_sib])
    columns = column_groups(
        place[3:], lag_bins, population, [corner], after(part, near_rows), groups
    )

    spot = jnp.stack([core * 2, core * 2 + 1, 2 - core * 2, 3 - core * 2]).astype(jnp.int32)
    shape = (2, 4, 2, 2, half, groups, rows)

    def products(position, pieces, held, ready):
        return product_rows(
            jnp.stack([position, jnp.int32(0)]).astype(jnp.int32),
            spot,
            population,
            [(piece, at) for piece in pieces for at in range(0, piece.shape[0], half)],
            half,
            [columns],
            0,
            held,
            shape,
            ready,
        )

    out = products(z, [own_rows], None, True)
    out_far_near = send(after(far_near, out), OUTWARD, "out_far_near")
    second = jnp.where(inside, far, after(out_far, out))
    second_sib = send(second, SIBLING, "second_sib")
    out = products(z ^ 1, [near_rows], out, True)
    out = products(jnp.where(low, 2, 1), [second, second_sib], out, False)
    third = jnp.where(inside, far_near, after(out_far_near, out))
    third_sib = send(third, SIBLING, "third_sib")
    out = products(jnp.where(low, 3, 0), [third, third_sib], out, False)
    return out.reshape(2, 8 * rows, groups, rows)


def solution(mesh):
    placed = (P(("row", "blk"), None), P(), P())
    line = mesh.shape["row"] == 4 and mesh.shape["blk"] == 8
    return jax.shard_map(
        line_shards if line else gathered_shards,
        mesh=mesh,
        in_specs=placed,
        out_specs=P(None, "row", None, "blk"),
        check_vma=False,
    )
```
